32 devices in a mesh: dp: 4 (over z), row: 4 (over y, x), col: 2 (over core).
Axes of the slice: x: 2, y: 2, z: 4, core: 2. Of those that a mesh axis runs over, the one named last changes fastest.
Arguments:
- layer_input: bfloat16 [768, 4096], P(('dp', 'col'), 'row'), may hold values from -6 to 6
- hidden_grad: bfloat16 [768, 14336], P(('dp', 'row'), 'col'), may hold values from -6 to 6
- gate_slots: bfloat16 [4, 2, 192, 128, 128], P('row', 'col', 'dp'), may hold values from -0.125 to 0.125
- up_slots: bfloat16 [4, 2, 192, 128, 128], P('row', 'col', 'dp'), may hold values from -0.125 to 0.125
- block_mask: int32 [32, 112], replicated, may hold values from 0 to 1, as said below
Outputs:
- input_grad: bfloat16 [768, 4096], P(('dp', 'col'), 'row')
- gate_slot_grad: float32 [4, 2, 192, 128, 128], P('row', 'col', 'dp')
- up_slot_grad: float32 [4, 2, 192, 128, 128], P('row', 'col', 'dp')
The draws below stay inside these ranges and needn't reach their ends.
Inputs may be any that keep to these rules, and one draw needn't show every extreme that they name: `block_mask`: every tile of 8 x 56 blocks keeps between 96 and 192 blocks; some tile keeps exactly 192, which tile depends on the draw.
All inputs are finite; a program needn't handle non-finite values.
Results may differ from the reference program's by a relative error of at most 0.022.
Values may be sent and summed in bfloat16 or wider, within the bound.
A program may use at most 128 MiB of HBM per device.

```python
import jax
import jax.numpy as jnp
from jax import lax

D = 4096
FF = 14336
BS = 128
TOK = 192
GRID_R = 4
GRID_C = 2
REPLICAS = 4
TOKENS = 768
NBR = 8
NBC = 56
NBT = 448
CAP = 192


def draw_block_mask(key, part):
    key_full, key_counts, key_perm = jax.random.split(jax.random.fold_in(key, 17), 3)
    tile_count = GRID_R * GRID_C
    counts = jax.random.randint(key_counts, (tile_count,), CAP // 2, CAP + 1)
    full_tile = jax.random.randint(key_full, (), 0, tile_count)
    counts = jnp.where(jnp.arange(tile_count) == full_tile, CAP, counts).astype(jnp.int32)
    tile_keys = jax.random.split(key_perm, tile_count)

    def one_tile(tile_key, kept_count):
        ordering = jax.random.permutation(tile_key, NBT)
        rank_of = jnp.zeros((NBT,), jnp.int32).at[ordering].set(jnp.arange(NBT, dtype=jnp.int32))
        return (rank_of < kept_count).astype(jnp.int32)
    kept_blocks = jax.vmap(one_tile)(tile_keys, counts)
    kept_blocks = kept_blocks.reshape(GRID_R, GRID_C, NBR, NBC).transpose(0, 2, 1, 3)
    return kept_blocks.reshape(GRID_R * NBR, GRID_C * NBC)


def steps_of(stream_key, extent, cuts, least, largest):
    gain = 1.0
    for axis_at, blocks in cuts:
        steps = jax.random.uniform(jax.random.fold_in(jax.random.fold_in(stream_key, 6), axis_at), (blocks,), jnp.float32, least / len(cuts), largest / len(cuts))
        gain = gain * jnp.repeat(jnp.exp(steps), extent[axis_at] // blocks).reshape((-1,) + (1,) * (len(extent) - 1 - axis_at))
    return gain


def normal_values(rng, shape, scale, limit, cuts=(), kind=jnp.bfloat16):
    factor_of = steps_of(rng, shape, cuts, -0.22, 0.18) if cuts else 1.0
    drawn = jax.random.normal(rng, shape, jnp.float32) * scale * factor_of
    return jnp.minimum(jnp.maximum(drawn, -limit), limit).astype(kind)


def setup_inputs(seed: int = 0) -> dict:
    keys = jax.random.split(jax.random.key(seed), 6)
    layer_input = normal_values(keys[0], (TOKENS, D), 1.0, 6.0, ((0, 8), (1, 4)))
    hidden_grad = normal_values(keys[1], (TOKENS, FF), 1.0, 6.0, ((0, 16), (1, 2)))
    gate_slots = normal_values(keys[2], (GRID_R, GRID_C, CAP, BS, BS), (D // 2) ** -0.5, 0.125, ((0, 4), (1, 2), (2, 4)))
    up_slots = normal_values(keys[3], (GRID_R, GRID_C, CAP, BS, BS), (D // 2) ** -0.5, 0.125, ((0, 4), (1, 2), (2, 4)))
    block_mask = draw_block_mask(jax.random.fold_in(keys[5], 71), 0)
    return {"layer_input": layer_input, "hidden_grad": hidden_grad, "gate_slots": gate_slots, "up_slots": up_slots, "block_mask": block_mask}


def rounded(array_in):
    return lax.optimization_barrier(array_in.astype(jnp.bfloat16)).astype(jnp.float32)

def tile_slots(block_mask):
    tile_mask = block_mask.reshape(GRID_R, NBR, GRID_C, NBC).transpose(0, 2, 1, 3).reshape(GRID_R * GRID_C, NBT)
    before = jnp.cumsum(tile_mask, axis=1) - tile_mask
    tile_ids = jnp.arange(GRID_R * GRID_C, dtype=jnp.int32)[:, None]
    where_slot = (tile_ids * CAP + jnp.where(tile_mask > 0, before, 0)).astype(jnp.int32)
    return (tile_mask, where_slot.reshape(-1))

def dense_weight(slot_blocks, tile_mask, where_slot):
    flat_slots = slot_blocks.reshape(GRID_R * GRID_C * CAP, BS, BS)
    blocks = jnp.take(flat_slots, where_slot, axis=0).reshape(GRID_R * GRID_C, NBT, BS, BS)
    blocks = blocks * tile_mask[:, :, None, None].astype(slot_blocks.dtype)
    blocks = blocks.reshape(GRID_R, GRID_C, NBR, NBC, BS, BS).transpose(0, 2, 4, 1, 3, 5)
    return blocks.reshape(D, FF).astype(jnp.float32)

def pack_grad(dense_grad, tile_mask, where_slot):
    blocks = dense_grad.reshape(GRID_R, NBR, BS, GRID_C, NBC, BS).transpose(0, 3, 1, 4, 2, 5)
    blocks = blocks.reshape(GRID_R * GRID_C, NBT, BS, BS) * tile_mask[:, :, None, None].astype(jnp.float32)
    packed = jnp.zeros((GRID_R * GRID_C * CAP, BS, BS), jnp.float32)
    packed = packed.at[where_slot].add(blocks.reshape(GRID_R * GRID_C * NBT, BS, BS))
    return packed.reshape(GRID_R, GRID_C, CAP, BS, BS)

def reference(layer_input, hidden_grad, gate_slots, up_slots, block_mask):
    highest = lax.Precision.HIGHEST
    tile_mask, where_slot = tile_slots(block_mask)
    gate_weight = dense_weight(gate_slots, tile_mask, where_slot)
    up_weight = dense_weight(up_slots, tile_mask, where_slot)
    inputs = layer_input.astype(jnp.float32)
    upstream = hidden_grad.astype(jnp.float32)
    feat_group = D // GRID_R
    gate = jnp.zeros((TOKENS, FF), jnp.float32)
    up_pre = jnp.zeros((TOKENS, FF), jnp.float32)
    for group_idx in range(GRID_R):
        low_row = group_idx * feat_group
        part_in = inputs[:, low_row:low_row + feat_group]
        gate = gate + rounded(jnp.dot(part_in, gate_weight[low_row:low_row + feat_group], precision=highest))
        up_pre = up_pre + rounded(jnp.dot(part_in, up_weight[low_row:low_row + feat_group], precision=highest))
    sigmoid_gate = jax.nn.sigmoid(gate)
    gate_grad = (upstream * up_pre * sigmoid_gate * (1.0 + gate * (1.0 - sigmoid_gate))).astype(jnp.bfloat16)
    up_grad = (upstream * gate * sigmoid_gate).astype(jnp.bfloat16)
    gate_gradf = gate_grad.astype(jnp.float32)
    up_gradf = up_grad.astype(jnp.float32)
    unit_group = FF // GRID_C
    input_sum = jnp.zeros((TOKENS, D), jnp.float32)
    for group_idx in range(GRID_C):
        low_col = group_idx * unit_group
        term = jnp.dot(gate_gradf[:, low_col:low_col + unit_group], gate_weight[:, low_col:low_col + unit_group].T, precision=highest)
        term = term + jnp.dot(up_gradf[:, low_col:low_col + unit_group], up_weight[:, low_col:low_col + unit_group].T, precision=highest)
        input_sum = input_sum + rounded(term)

    def add_replica(accum, replica_items):
        block_in, block_gate, block_up = replica_items
        next_gate = accum[0] + rounded(jnp.dot(block_in.T, block_gate, precision=highest))
        next_up = accum[1] + rounded(jnp.dot(block_in.T, block_up, precision=highest))
        return ((next_gate, next_up), None)
    zero_dense = jnp.zeros((D, FF), jnp.float32)
    replica_items = (inputs.reshape(REPLICAS, TOK, D), gate_gradf.reshape(REPLICAS, TOK, FF), up_gradf.reshape(REPLICAS, TOK, FF))
    (gate_acc, up_acc), unused = lax.scan(add_replica, (zero_dense, zero_dense), replica_items)
    gate_slot_grad = pack_grad(gate_acc / REPLICAS, tile_mask, where_slot)
    up_slot_grad = pack_grad(up_acc / REPLICAS, tile_mask, where_slot)
    return (input_sum.astype(jnp.bfloat16), gate_slot_grad, up_slot_grad)
```

```python
import functools

import jax
import jax.numpy as jnp
from jax import lax
from jax.experimental import pallas as pl
from jax.experimental.pallas import tpu as pltpu
from jax.sharding import PartitionSpec as P

MESH = pl.DeviceIdType.MESH


def slot_maps(block_mask, tile_rows, tile_cols, local_cap):
    row_first = lax.axis_index("row") * tile_rows
    col_first = lax.axis_index("col") * tile_cols
    tile_mask = lax.dynamic_slice(block_mask, (row_first, col_first), (tile_rows, tile_cols))
    blocks = tile_rows * tile_cols
    flat_mask = tile_mask.reshape(blocks)
    ids = jnp.arange(blocks, dtype=jnp.int32)
    before = jnp.sum(jnp.where(ids[None, :] < ids[:, None], flat_mask[None, :], 0), axis=1)
    local = before - lax.axis_index("dp") * local_cap
    here = (flat_mask > 0) & (local >= 0) & (local < local_cap)
    where_slot = jnp.where(here, local, local_cap).astype(jnp.int32)
    slot_ids = jnp.arange(local_cap, dtype=jnp.int32)
    chosen = (where_slot[:, None] == slot_ids[None, :]).astype(jnp.int32)
    slot_block = jnp.sum(chosen * ids[:, None], axis=0)
    live = jnp.sum(chosen, axis=0)
    return where_slot, slot_block // tile_cols, slot_block % tile_cols, live


def kernel(
    sizes, where_ref, tok_ref, w_ref, hg_ref,
    dx_ref, grads_ref,
    grads, part, recv1, recv2, recvz, dense, dx_acc,
    s1, r1, s2, r2, sz, rz, sa, ra, sb, rb, sc, rc, so,
):
    n_row, n_dp, n_chunks, tile_rows, lag, ring, part_ring = sizes
    bs = hg_ref.shape[-1]
    me_row = lax.axis_index("row")
    me_dp = lax.axis_index("dp")
    low, high = me_row % 2, me_row // 2
    px = high * 2 + (1 - low)
    py = (1 - high) * 2 + low
    diag = 3 - me_row

    barrier = pltpu.get_barrier_semaphore()
    for other in (px, py):
        pl.semaphore_signal(barrier, inc=1, device_id={"row": other}, device_id_type=MESH)
    for step in range(1, n_dp):
        pl.semaphore_signal(barrier, inc=1, device_id={"dp": (me_dp + step) % n_dp}, device_id_type=MESH)
    pl.semaphore_wait(barrier, 2 + n_dp - 1)

    def send(src, dst, s, r, device):
        return pltpu.make_async_remote_copy(
            src_ref=src, dst_ref=dst, send_sem=s, recv_sem=r, device_id=device, device_id_type=MESH
        )

    def partners(c):
        q = c % 2
        return q * py + (1 - q) * px, q * px + (1 - q) * py

    def build(c):
        for r in range(tile_rows):
            dense[r * bs : (r + 1) * bs, :] = w_ref[where_ref[r * n_chunks + c]]

    def first_copies(c):
        p1, p2 = partners(c)
        slot, k = c % part_ring, c % ring
        return [
            send(part.at[slot, p1], recv1.at[k, 0], s1.at[k, 0], r1.at[k, 0], {"row": p1}),
            send(part.at[slot, diag], recv1.at[k, 1], s1.at[k, 1], r1.at[k, 1], {"row": p1}),
        ]

    def second_copy(c):
        p1, p2 = partners(c)
        k = c % ring
        return send(recv1.at[k, 1], recv2.at[k], s2.at[k], r2.at[k], {"row": p2})

    def depth_copies(c):
        k = c % ring
        out = []
        for step in range(1, n_dp):
            other = (me_dp + step) % n_dp
            out.append(send(
                recv2.at[k, other], recvz.at[k, step - 1], sz.at[k, step - 1], rz.at[k, step - 1], {"dp": other}
            ))
        return out

    def depth_gathers(c):
        k = c % ring
        mine = grads.at[c, me_row, me_dp]
        return [
            send(mine, mine, sa.at[k, step - 1], ra.at[k, step - 1], {"dp": (me_dp + step) % n_dp})
            for step in range(1, n_dp)
        ]

    def near_gather(c):
        p1, p2 = partners(c)
        k = c % ring
        return send(grads.at[c, me_row], grads.at[c, me_row], sb.at[k], rb.at[k], {"row": p2})

    def far_gathers(c):
        p1, p2 = partners(c)
        k = c % ring
        return [
            send(grads.at[c, me_row], grads.at[c, me_row], sc.at[k, 0], rc.at[k, 0], {"row": p1}),
            send(grads.at[c, p2], grads.at[c, p2], sc.at[k, 1], rc.at[k, 1], {"row": p1}),
        ]

    def keep(c):
        return pltpu.make_async_copy(grads.at[c], grads_ref.at[c], so.at[c])

    dx_acc[...] = jnp.zeros_like(dx_acc)

    def iteration(t, carry):
        def at(stage, body):
            c = t - lag * stage

            @pl.when((c >= 0) & (c < n_chunks))
            def _():
                body(c)

        def stage1(c):
            for copy in first_copies(c):
                copy.wait()
            p1, p2 = partners(c)
            slot, k = c % part_ring, c % ring
            for i, r in ((1, p2), (0, me_row)):
                recv1[k, i] = (
                    part[slot, r].astype(jnp.float32) + recv1[k, i].astype(jnp.float32)
                ).astype(jnp.bfloat16)
                if i == 1:
                    second_copy(c).start()

        def stage2(c):
            second_copy(c).wait()
            k = c % ring
            recv2[k] = (recv1[k, 0].astype(jnp.float32) + recv2[k].astype(jnp.float32)).astype(jnp.bfloat16)
            for copy in depth_copies(c):
                copy.start()

        def stage3(c):
            for copy in depth_copies(c):
                copy.wait()
            k = c % ring
            total = recv2[k, me_dp].astype(jnp.float32)
            for step in range(n_dp - 1):
                total = total + recvz[k, step].astype(jnp.float32)
            gate, up = total[:, :bs], total[:, bs:]
            upstream = hg_ref[c].astype(jnp.float32)
            sig = jax.nn.sigmoid(gate)
            grads[c, me_row, me_dp] = jnp.concatenate(
                [upstream * up * sig * (1.0 + gate * (1.0 - sig)), upstream * gate * sig], axis=1
            ).astype(jnp.bfloat16)
            for copy in depth_gathers(c):
                copy.start()

        def stage4(c):
            for copy in depth_gathers(c):
                copy.wait()
            near_gather(c).start()

        def stage5(c):
            near_gather(c).wait()
            for copy in far_gathers(c):
                copy.start()

        def stage6(c):
            for copy in far_gathers(c):
                copy.wait()
            keep(c).start()
            build(c)

            def rows(r, carry):
                g = grads[c, r].reshape(-1, 2 * bs)
                dx_acc[r] += lax.dot_general(
                    g, dense[...], (((1,), (1,)), ((), ())), preferred_element_type=jnp.float32
                )
                return carry

            lax.fori_loop(0, n_row, rows, 0)

        def stage0(c):
            build(c)
            slot = c % part_ring

            def rows(r, carry):
                part[slot, r] = (
                    jnp.dot(tok_ref[r], dense[...], preferred_element_type=jnp.float32)
                    .astype(jnp.bfloat16)
                    .reshape(part.shape[2:])
                )
                return carry

            lax.fori_loop(0, n_row, rows, 0)
            for copy in first_copies(c):
                copy.start()

        at(5, stage5)
        at(4, stage4)
        at(3, stage3)
        at(2, stage2)
        at(1, stage1)
        at(6, stage6)
        at(0, stage0)
        return carry

    lax.fori_loop(0, n_chunks + 6 * lag, iteration, 0)

    def finish(r, carry):
        dx_ref[r] = dx_acc[r].astype(jnp.bfloat16)
        return carry

    lax.fori_loop(0, n_row, finish, 0)

    def kept(c, carry):
        keep(c).wait()
        return carry

    lax.fori_loop(0, n_chunks, kept, 0)


def slot_kernel(srow_ref, scol_ref, scale_ref, tok_ref, *refs):
    *grad_refs, gate_ref, up_ref = refs
    bs = gate_ref.shape[-1]
    first = pl.program_id(0) * len(grad_refs)
    for i, grad_ref in enumerate(grad_refs):
        total = jnp.dot(tok_ref[srow_ref[first + i]], grad_ref[0], preferred_element_type=jnp.float32)
        total = total * scale_ref[first + i]
        gate_ref[i] = total[:, :bs]
        up_ref[i] = total[:, bs:]


def slot_grads(srow, scol, scale, tok_blocks, grads):
    cap = srow.shape[0]
    bs, tokens = tok_blocks.shape[1:]
    each = next(n for n in (4, 3, 2, 1) if cap % n == 0)
    return pl.pallas_call(
        slot_kernel,
        grid_spec=pltpu.PrefetchScalarGridSpec(
            num_scalar_prefetch=3,
            grid=(cap // each,),
            in_specs=[pl.BlockSpec(tok_blocks.shape, lambda s, *_: (0, 0, 0))]
            + [
                pl.BlockSpec((1, tokens, 2 * bs), lambda s, row, col, scale, i=i: (col[s * each + i], 0, 0))
                for i in range(each)
            ],
            out_specs=[pl.BlockSpec((each, bs, bs), lambda s, *_: (s, 0, 0))] * 2,
        ),
        out_shape=[jax.ShapeDtypeStruct((cap, bs, bs), jnp.float32)] * 2,
        compiler_params=pltpu.CompilerParams(vmem_limit_bytes=48 * 2**20),
        cost_estimate=pl.CostEstimate(
            flops=cap * tokens * bs * bs * 4, bytes_accessed=cap * tokens * bs * 4 + cap * bs * bs * 8, transcendentals=0
        ),
    )(srow, scol, scale, tok_blocks, *[grads] * each)


def on_device(layer_input, hidden_grad, gate_slots, up_slots, block_mask):
    gate_local, up_local = gate_slots[0, 0], up_slots[0, 0]
    local_cap, bs = gate_local.shape[0], gate_local.shape[-1]
    n_dp, n_row = lax.axis_size("dp"), lax.axis_size("row")
    feat = layer_input.shape[1]
    rows_each, units = hidden_grad.shape
    tile_rows, tile_cols = feat // bs, units // bs
    where_slot, srow, scol, live = slot_maps(block_mask, tile_rows, tile_cols, local_cap)
    scale = live.astype(jnp.float32) / n_dp
    tokens = lax.all_gather(layer_input, ("dp", "col"), axis=0, tiled=True)
    tokens = (
        tokens.reshape(n_dp, n_row, rows_each, feat).transpose(1, 0, 2, 3).reshape(n_row, n_dp * rows_each, feat)
    )
    weights = jnp.pad(jnp.concatenate([gate_local, up_local], axis=2), ((0, 1), (0, 0), (0, 0)))
    upstream = hidden_grad.reshape(rows_each, tile_cols, bs).transpose(1, 0, 2)
    lag = 2 if n_dp <= 4 else 1
    ring = 6 * lag + 2
    part_ring = lag + 1
    sizes = (n_row, n_dp, tile_cols, tile_rows, lag, ring, part_ring)
    wide = 2 * bs
    bf = jnp.bfloat16
    dma = pltpu.SemaphoreType.DMA
    vm = pl.BlockSpec(memory_space=pltpu.VMEM)
    sm = pl.BlockSpec(memory_space=pltpu.SMEM)
    dx, grads = pl.pallas_call(
        functools.partial(kernel, sizes),
        out_shape=(
            jax.ShapeDtypeStruct((n_row, n_dp * rows_each, feat), bf),
            jax.ShapeDtypeStruct((tile_cols, n_row, n_dp, rows_each, wide), bf),
        ),
        in_specs=[sm, vm, vm, vm],
        out_specs=(vm, pl.BlockSpec(memory_space=pl.ANY)),
        scratch_shapes=[
            pltpu.VMEM((tile_cols, n_row, n_dp, rows_each, wide), bf),
            pltpu.VMEM((part_ring, n_row, n_dp, rows_each, wide), bf),
            pltpu.VMEM((ring, 2, n_dp, rows_each, wide), bf),
            pltpu.VMEM((ring, n_dp, rows_each, wide), bf),
            pltpu.VMEM((ring, n_dp - 1, rows_each, wide), bf),
            pltpu.VMEM((feat, wide), bf),
            pltpu.VMEM((n_row, n_dp * rows_each, feat), jnp.float32),
            dma((ring, 2)), dma((ring, 2)),
            dma((ring,)), dma((ring,)),
            dma((ring, n_dp - 1)), dma((ring, n_dp - 1)),
            dma((ring, n_dp - 1)), dma((ring, n_dp - 1)),
            dma((ring,)), dma((ring,)),
            dma((ring, 2)), dma((ring, 2)),
            dma((tile_cols,)),
        ],
        compiler_params=pltpu.CompilerParams(
            collective_id=0, has_side_effects=True, vmem_limit_bytes=63 * 2**20
        ),
    )(where_slot, tokens, weights, upstream)
    dx = dx.reshape(n_row, n_dp, rows_each, feat).transpose(1, 0, 2, 3).reshape(-1, feat)
    tok_blocks = tokens.reshape(-1, tile_rows, bs).transpose(1, 2, 0)
    gate_out, up_out = slot_grads(srow, scol, scale, tok_blocks, grads.reshape(tile_cols, -1, wide))
    input_sum = lax.psum_scatter(dx, ("dp", "col"), scatter_dimension=0, tiled=True)
    return (input_sum, gate_out[None, None], up_out[None, None])


def solution(mesh):
    return jax.shard_map(
        on_device,
        mesh=mesh,
        in_specs=(
            P(("dp", "col"), "row"),
            P(("dp", "row"), "col"),
            P("row", "col", "dp", None, None),
            P("row", "col", "dp", None, None),
            P(),
        ),
        out_specs=(
            P(("dp", "col"), "row"),
            P("row", "col", "dp", None, None),
            P("row", "col", "dp", None, None),
        ),
        check_vma=False,
    )
```

```python
import functools

import jax
import jax.numpy as jnp
from jax import lax
from jax.experimental import pallas as pl
from jax.experimental.pallas import tpu as pltpu
from jax.sharding import PartitionSpec as P

MESH = pl.DeviceIdType.MESH


def slot_maps(block_mask, tile_rows, tile_cols, local_cap):
    row_first = lax.axis_index("row") * tile_rows
    col_first = lax.axis_index("col") * tile_cols
    tile_mask = lax.dynamic_slice(block_mask, (row_first, col_first), (tile_rows, tile_cols))
    blocks = tile_rows * tile_cols
    flat_mask = tile_mask.reshape(blocks)
    ids = jnp.arange(blocks, dtype=jnp.int32)
    before = jnp.sum(jnp.where(ids[None, :] < ids[:, None], flat_mask[None, :], 0), axis=1)
    local = before - lax.axis_index("dp") * local_cap
    here = (flat_mask > 0) & (local >= 0) & (local < local_cap)
    where_slot = jnp.where(here, local, local_cap).astype(jnp.int32)
    slot_ids = jnp.arange(local_cap, dtype=jnp.int32)
    chosen = (where_slot[:, None] == slot_ids[None, :]).astype(jnp.int32)
    slot_block = jnp.sum(chosen * ids[:, None], axis=0)
    live = jnp.sum(chosen, axis=0)
    return where_slot, slot_block // tile_cols, slot_block % tile_cols, live


def kernel(
    sizes, where_ref, tok_ref, w_ref, hg_ref,
    dx_ref, grads_ref,
    grads, part, recv1, recv2, recvz, dense, dx_acc,
    s1, r1, s2, r2, sz, rz, sa, ra, sb, rb, sc, rc, so,
):
    n_row, n_dp, n_chunks, tile_rows, lag, ring, part_ring = sizes
    bs = hg_ref.shape[-1]
    me_row = lax.axis_index("row")
    me_dp = lax.axis_index("dp")
    low, high = me_row % 2, me_row // 2
    px = high * 2 + (1 - low)
    py = (1 - high) * 2 + low
    diag = 3 - me_row

    barrier = pltpu.get_barrier_semaphore()
    for other in (px, py):
        pl.semaphore_signal(barrier, inc=1, device_id={"row": other}, device_id_type=MESH)
    for step in range(1, n_dp):
        pl.semaphore_signal(barrier, inc=1, device_id={"dp": (me_dp + step) % n_dp}, device_id_type=MESH)
    pl.semaphore_wait(barrier, 2 + n_dp - 1)

    def send(src, dst, s, r, device):
        return pltpu.make_async_remote_copy(
            src_ref=src, dst_ref=dst, send_sem=s, recv_sem=r, device_id=device, device_id_type=MESH
        )

    def partners(c):
        q = c % 2
        return q * py + (1 - q) * px, q * px + (1 - q) * py

    def build(c):
        for r in range(tile_rows):
            dense[r * bs : (r + 1) * bs, :] = w_ref[where_ref[r * n_chunks + c]]

    def first_copies(c):
        p1, p2 = partners(c)
        slot, k = c % part_ring, c % ring
        return [
            send(part.at[slot, p1], recv1.at[k, 0], s1.at[k, 0], r1.at[k, 0], {"row": p1}),
            send(part.at[slot, diag], recv1.at[k, 1], s1.at[k, 1], r1.at[k, 1], {"row": p1}),
        ]

    def second_copy(c):
        p1, p2 = partners(c)
        k = c % ring
        return send(recv1.at[k, 1], recv2.at[k], s2.at[k], r2.at[k], {"row": p2})

    def depth_copies(c):
        k = c % ring
        out = []
        for step in range(1, n_dp):
            other = (me_dp + step) % n_dp
            out.append(send(
                recv2.at[k, other], recvz.at[k, step - 1], sz.at[k, step - 1], rz.at[k, step - 1], {"dp": other}
            ))
        return out

    def depth_gathers(c):
        k = c % ring
        mine = grads.at[c, me_row, me_dp]
        return [
            send(mine, mine, sa.at[k, step - 1], ra.at[k, step - 1], {"dp": (me_dp + step) % n_dp})
            for step in range(1, n_dp)
        ]

    def near_gather(c):
        p1, p2 = partners(c)
        k = c % ring
        return send(grads.at[c, me_row], grads.at[c, me_row], sb.at[k], rb.at[k], {"row": p2})

    def far_gathers(c):
        p1, p2 = partners(c)
        k = c % ring
        return [
            send(grads.at[c, me_row], grads.at[c, me_row], sc.at[k, 0], rc.at[k, 0], {"row": p1}),
            send(grads.at[c, p2], grads.at[c, p2], sc.at[k, 1], rc.at[k, 1], {"row": p1}),
        ]

    def keep(c):
        return pltpu.make_async_copy(grads.at[c], grads_ref.at[c], so.at[c])

    dx_acc[...] = jnp.zeros_like(dx_acc)

    def iteration(t, carry):
        def at(stage, body):
            c = t - lag * stage

            @pl.when((c >= 0) & (c < n_chunks))
            def _():
                body(c)

        def stage1(c):
            for copy in first_copies(c):
                copy.wait()
            p1, p2 = partners(c)
            slot, k = c % part_ring, c % ring
            for i, r in ((1, p2), (0, me_row)):
                recv1[k, i] = (
                    part[slot, r].astype(jnp.float32) + recv1[k, i].astype(jnp.float32)
                ).astype(jnp.bfloat16)
                if i == 1:
                    second_copy(c).start()

        def stage2(c):
            second_copy(c).wait()
            k = c % ring
            recv2[k] = (recv1[k, 0].astype(jnp.float32) + recv2[k].astype(jnp.float32)).astype(jnp.bfloat16)
            for copy in depth_copies(c):
                copy.start()

        def stage3(c):
            for copy in depth_copies(c):
                copy.wait()
            k = c % ring
            total = recv2[k, me_dp].astype(jnp.float32)
            for step in range(n_dp - 1):
                total = total + recvz[k, step].astype(jnp.float32)
            gate, up = total[:, :bs], total[:, bs:]
            upstream = hg_ref[c].astype(jnp.float32)
            sig = jax.nn.sigmoid(gate)
            grads[c, me_row, me_dp] = jnp.concatenate(
                [upstream * up * sig * (1.0 + gate * (1.0 - sig)), upstream * gate * sig], axis=1
            ).astype(jnp.bfloat16)
            for copy in depth_gathers(c):
                copy.start()

        def stage4(c):
            for copy in depth_gathers(c):
                copy.wait()
            near_gather(c).start()

        def stage5(c):
            near_gather(c).wait()
            for copy in far_gathers(c):
                copy.start()

        def stage6(c):
            for copy in far_gathers(c):
                copy.wait()
            keep(c).start()
            build(c)

            def rows(r, carry):
                g = grads[c, r].reshape(-1, 2 * bs)
                dx_acc[r] += lax.dot_general(
                    g, dense[...], (((1,), (1,)), ((), ())), preferred_element_type=jnp.float32
                )
                return carry

            lax.fori_loop(0, n_row, rows, 0)

        def stage0(c):
            build(c)
            slot = c % part_ring

            def rows(r, carry):
                part[slot, r] = (
                    jnp.dot(tok_ref[:, r].reshape(-1, tok_ref.shape[-1]), dense[...], preferred_element_type=jnp.float32)
                    .astype(jnp.bfloat16)
                    .reshape(part.shape[2:])
                )
                return carry

            lax.fori_loop(0, n_row, rows, 0)
            for copy in first_copies(c):
                copy.start()

        at(5, stage5)
        at(4, stage4)
        at(3, stage3)
        at(2, stage2)
        at(1, stage1)
        at(6, stage6)
        at(0, stage0)
        return carry

    lax.fori_loop(0, n_chunks + 6 * lag, iteration, 0)

    def finish(r, carry):
        dx_ref[:, r] = dx_acc[r].astype(jnp.bfloat16).reshape(dx_ref.shape[:1] + dx_ref.shape[2:])
        return carry

    lax.fori_loop(0, n_row, finish, 0)

    def kept(c, carry):
        keep(c).wait()
        return carry

    lax.fori_loop(0, n_chunks, kept, 0)


def slot_kernel(srow_ref, scol_ref, scale_ref, tok_ref, *refs):
    *grad_refs, gate_ref, up_ref = refs
    bs = gate_ref.shape[-1]
    first = pl.program_id(0) * len(grad_refs)
    for i, grad_ref in enumerate(grad_refs):
        total = jnp.dot(tok_ref[srow_ref[first + i]], grad_ref[0], preferred_element_type=jnp.float32)
        total = total * scale_ref[first + i]
        gate_ref[i] = total[:, :bs]
        up_ref[i] = total[:, bs:]


def slot_grads(srow, scol, scale, tok_blocks, grads):
    cap = srow.shape[0]
    bs, tokens = tok_blocks.shape[1:]
    each = next(n for n in (4, 3, 2, 1) if cap % n == 0)
    return pl.pallas_call(
        slot_kernel,
        grid_spec=pltpu.PrefetchScalarGridSpec(
            num_scalar_prefetch=3,
            grid=(cap // each,),
            in_specs=[pl.BlockSpec(tok_blocks.shape, lambda s, *_: (0, 0, 0))]
            + [
                pl.BlockSpec((1, tokens, 2 * bs), lambda s, row, col, scale, i=i: (col[s * each + i], 0, 0))
                for i in range(each)
            ],
            out_specs=[pl.BlockSpec((each, bs, bs), lambda s, *_: (s, 0, 0))] * 2,
        ),
        out_shape=[jax.ShapeDtypeStruct((cap, bs, bs), jnp.float32)] * 2,
        compiler_params=pltpu.CompilerParams(vmem_limit_bytes=48 * 2**20),
        cost_estimate=pl.CostEstimate(
            flops=cap * tokens * bs * bs * 4, bytes_accessed=cap * tokens * bs * 4 + cap * bs * bs * 8, transcendentals=0
        ),
    )(srow, scol, scale, tok_blocks, *[grads] * each)


def on_device(layer_input, hidden_grad, gate_slots, up_slots, block_mask):
    gate_local, up_local = gate_slots[0, 0], up_slots[0, 0]
    local_cap, bs = gate_local.shape[0], gate_local.shape[-1]
    n_dp, n_row = lax.axis_size("dp"), lax.axis_size("row")
    feat = layer_input.shape[1]
    rows_each, units = hidden_grad.shape
    tile_rows, tile_cols = feat // bs, units // bs
    where_slot, srow, scol, live = slot_maps(block_mask, tile_rows, tile_cols, local_cap)
    scale = live.astype(jnp.float32) / n_dp
    tokens = lax.all_gather(layer_input, ("dp", "col"), axis=0, tiled=True)
    tokens = tokens.reshape(n_dp, n_row, rows_each, feat)
    weights = jnp.pad(jnp.concatenate([gate_local, up_local], axis=2), ((0, 1), (0, 0), (0, 0)))
    upstream = hidden_grad.reshape(rows_each, tile_cols, bs).transpose(1, 0, 2)
    lag = 3 if n_dp <= 4 else 1
    ring = 6 * lag + 2
    part_ring = lag + 1
    sizes = (n_row, n_dp, tile_cols, tile_rows, lag, ring, part_ring)
    wide = 2 * bs
    bf = jnp.bfloat16
    dma = pltpu.SemaphoreType.DMA
    vm = pl.BlockSpec(memory_space=pltpu.VMEM)
    sm = pl.BlockSpec(memory_space=pltpu.SMEM)
    dx, grads = pl.pallas_call(
        functools.partial(kernel, sizes),
        out_shape=(
            jax.ShapeDtypeStruct((n_dp, n_row, rows_each, feat), bf),
            jax.ShapeDtypeStruct((tile_cols, n_row, n_dp, rows_each, wide), bf),
        ),
        in_specs=[sm, vm, vm, vm],
        out_specs=(vm, pl.BlockSpec(memory_space=pl.ANY)),
        scratch_shapes=[
            pltpu.VMEM((tile_cols, n_row, n_dp, rows_each, wide), bf),
            pltpu.VMEM((part_ring, n_row, n_dp, rows_each, wide), bf),
            pltpu.VMEM((ring, 2, n_dp, rows_each, wide), bf),
            pltpu.VMEM((ring, n_dp, rows_each, wide), bf),
            pltpu.VMEM((ring, n_dp - 1, rows_each, wide), bf),
            pltpu.VMEM((feat, wide), bf),
            pltpu.VMEM((n_row, n_dp * rows_each, feat), jnp.float32),
            dma((ring, 2)), dma((ring, 2)),
            dma((ring,)), dma((ring,)),
            dma((ring, n_dp - 1)), dma((ring, n_dp - 1)),
            dma((ring, n_dp - 1)), dma((ring, n_dp - 1)),
            dma((ring,)), dma((ring,)),
            dma((ring, 2)), dma((ring, 2)),
            dma((tile_cols,)),
        ],
        compiler_params=pltpu.CompilerParams(
            collective_id=0, has_side_effects=True, vmem_limit_bytes=63 * 2**20
        ),
    )(where_slot, tokens, weights, upstream)
    tok_blocks = tokens.reshape(n_dp, n_row, rows_each, tile_rows, bs).transpose(3, 4, 1, 0, 2)
    tok_blocks = tok_blocks.reshape(tile_rows, bs, -1)
    gate_out, up_out = slot_grads(srow, scol, scale, tok_blocks, grads.reshape(tile_cols, -1, wide))
    input_sum = lax.psum_scatter(dx.reshape(-1, feat), ("dp", "col"), scatter_dimension=0, tiled=True)
    return (input_sum, gate_out[None, None], up_out[None, None])


def solution(mesh):
    return jax.shard_map(
        on_device,
        mesh=mesh,
        in_specs=(
            P(("dp", "col"), "row"),
            P(("dp", "row"), "col"),
            P("row", "col", "dp", None, None),
            P("row", "col", "dp", None, None),
            P(),
        ),
        out_specs=(
            P(("dp", "col"), "row"),
            P("row", "col", "dp", None, None),
            P("row", "col", "dp", None, None),
        ),
        check_vma=False,
    )
```
